512 devices in a mesh: chan: 32 (over x, z_lo, core), bl: 16 (over z_hi, y).
Axes of the slice: x: 4, y: 8, z: 8 (z_hi: 2, z_lo: 4; z = z_hi * 4 + z_lo), core: 2. Of those that a mesh axis runs over, the one named last changes fastest.
Arguments:
- gains: float32 [4096, 512], P('chan'), may hold values from -6 to 6
- consensus: float32 [4096, 512], P('chan'), may hold values from -6 to 6
- dual: float32 [4096, 512], P('chan'), may hold values from -3 to 3
- coherence: bfloat16 [4096, 32768], P('chan', 'bl'), may hold values from -1.5 to 1.5
- visibility: float32 [1024, 32768], P('chan', 'bl'), may hold values from -6 to 6
- stations: int32 [2, 32768], P(None, 'bl'), may hold values from 0 to 511, as said below
Outputs:
- gains_out: float32 [4096, 512], P('chan')
- consensus_out: float32 [4096, 512], P('chan')
- dual_out: float32 [4096, 512], P('chan')
The draws below stay inside these ranges and needn't reach their ends.
Inputs may be any that keep to these rules, and one draw needn't show every extreme that they name: Station indices of every baseline; the two stations of a baseline differ.
All inputs are finite; a program needn't handle non-finite values.
Results may differ from the reference program's by a relative error of at most 0.0003.
Values sent between devices are 32-bit elements; how exact they have to be, the bound alone decides.
A program may use at most 64 MiB of HBM per device.

```python
import jax
import jax.numpy as jnp
from jax import lax

ANTENNA_SITES = 512
SKY_DIRECTIONS = 4
ITERS = 2
FREQUENCY_BINS = 256
BASELINE_PAIRS = 32768


def draw_stations(key, part):
    key = jax.random.fold_in(key, 7)
    initial_key, secondary_key = jax.random.split(key)
    nearby_index = jax.random.randint(initial_key, (BASELINE_PAIRS,), 0, ANTENNA_SITES)
    shift_amount = jax.random.randint(secondary_key, (BASELINE_PAIRS,), 1, ANTENNA_SITES)
    nearby_index = nearby_index.at[0].set(ANTENNA_SITES - 1)
    nearby_index = nearby_index.at[1].set(0)
    far = (nearby_index + shift_amount) % ANTENNA_SITES
    return jnp.stack([nearby_index, far]).astype(jnp.int32)


def levels(key, shape, shards, smallest, largest):
    loudness, own = 1.0, jax.random.fold_in(key, 6)
    for dim, parts in shards:
        heights = jnp.exp(jax.random.uniform(jax.random.fold_in(own, dim), (parts,), jnp.float32, smallest / len(shards), largest / len(shards)))
        loudness = loudness * jnp.repeat(heights, shape[dim] // parts).reshape([-1 if axis == dim else 1 for axis in range(len(shape))])
    return loudness


def normal_values(rng, shape, deviation, most, pieces=(), kind=jnp.bfloat16):
    result = deviation * jax.random.normal(rng, shape, jnp.float32)
    if pieces:
        result = result * levels(rng, shape, pieces, -0.22, 0.18)
    return jnp.clip(result, -most, most).astype(kind)


def setup_inputs(seed: int = 0) -> dict:
    splits = jax.random.split(jax.random.key(seed), 7)
    return {
        "gains": normal_values(splits[0], (FREQUENCY_BINS * SKY_DIRECTIONS * 4, ANTENNA_SITES), 1.0, 6.0, ((0, 32),), jnp.float32),
        "consensus": normal_values(splits[1], (FREQUENCY_BINS * SKY_DIRECTIONS * 4, ANTENNA_SITES), 1.0, 6.0, ((0, 32),), jnp.float32),
        "dual": normal_values(splits[2], (FREQUENCY_BINS * SKY_DIRECTIONS * 4, ANTENNA_SITES), 0.5, 3.0, ((0, 32),), jnp.float32),
        "coherence": normal_values(splits[3], (FREQUENCY_BINS * SKY_DIRECTIONS * 4, BASELINE_PAIRS), 0.25, 1.5, ((0, 32), (1, 16))),
        "visibility": normal_values(splits[4], (FREQUENCY_BINS * 4, BASELINE_PAIRS), 1.0, 6.0, ((0, 32), (1, 16)), jnp.float32),
        "stations": draw_stations(jax.random.fold_in(splits[6], 71), 0),
    }


MU = 0.02
RHO = 25.0

def poly_basis(count):
    place = jnp.arange(count).astype(jnp.float32)
    level = (2.0 * place - (count - 1)) / count
    columns = []
    for power in range(4):
        vector = level ** power
        for prior in columns:
            vector = vector - jnp.sum(prior * vector) * prior
        vector = vector / jnp.sqrt(jnp.sum(vector * vector))
        columns.append(vector)
    return jnp.stack(columns, axis=1)

def pair_terms(nearby_index, far, coher, observed):
    width = nearby_index.shape[-1]
    first = nearby_index.reshape(-1, SKY_DIRECTIONS, 2, 2, width)
    second = far.reshape(-1, SKY_DIRECTIONS, 2, 2, width)
    model = coher.reshape(-1, SKY_DIRECTIONS, 2, 2, width)
    seen = observed.reshape(-1, 2, 2, width)
    ar, ai = (first[:, :, :, 0], first[:, :, :, 1])
    dr, di = (second[:, :, :, 0], second[:, :, :, 1])
    cr, ci = (model[:, :, :, 0], model[:, :, :, 1])
    er = cr * dr + ci * di
    ei = ci * dr - cr * di
    rr = (seen[:, :, 0] - lax.optimization_barrier(jnp.sum(ar * er - ai * ei, axis=1)))[:, None]
    ri = (seen[:, :, 1] - lax.optimization_barrier(jnp.sum(ar * ei + ai * er, axis=1)))[:, None]
    fr = ar * cr - ai * ci
    fi = ar * ci + ai * cr
    near_term = jnp.stack([-(rr * er + ri * ei), -(ri * er - rr * ei)], axis=3)
    far_term = jnp.stack([-(rr * fr + ri * fi), -(rr * fi - ri * fr)], axis=3)
    return (near_term.reshape(-1, width), far_term.reshape(-1, width))

def reference(gains, consensus, dual, coherence, visibility, stations):
    count = gains.shape[1]
    chans = gains.shape[0] // (SKY_DIRECTIONS * 4)
    near_ids = stations[0]
    far_ids = stations[1]
    basis = poly_basis(chans)
    high = lax.Precision.HIGHEST

    def one_channel(items):
        table, coher, observed = items
        nearby_index = jnp.take(table, near_ids, axis=1)
        far = jnp.take(table, far_ids, axis=1)
        near_term, far_term = pair_terms(nearby_index, far, coher.astype(jnp.float32), observed)
        total = jax.ops.segment_sum(near_term.T, near_ids, count) + jax.ops.segment_sum(far_term.T, far_ids, count)
        return total.T
    coher_all = coherence.reshape(chans, SKY_DIRECTIONS * 4, -1)
    seen_all = visibility.reshape(chans, 4, -1)
    for sweep in range(ITERS):
        grad = lax.map(one_channel, (gains.reshape(chans, SKY_DIRECTIONS * 4, count), coher_all, seen_all))
        grad = grad.reshape(chans * SKY_DIRECTIONS * 4, count)
        gains = gains - MU * (grad + RHO * (gains - consensus + dual))
        flat = (gains + dual).reshape(chans, SKY_DIRECTIONS * 4 * count)
        weights = jnp.dot(basis.T, flat, precision=high)
        consensus = jnp.dot(basis, weights, precision=high).reshape(chans * SKY_DIRECTIONS * 4, count)
        dual = dual + gains - consensus
    return (gains, consensus, dual)
```

```python
import functools

import jax
import jax.numpy as jnp
import numpy as np
from jax import lax
from jax.experimental import pallas as pl
from jax.experimental.pallas import tpu as pltpu
from jax.sharding import PartitionSpec as P

SKY_DIRECTIONS = 4
ITERS = 2
MU = 0.02
RHO = 25.0

CH = 8
ROWS = 8
MESH = pl.DeviceIdType.MESH
FAR_FIRST = (4, 3, 5, 2, 6, 1, 7)
XC_FAR_FIRST = ((2, 1), (2, 0), (1, 1), (3, 1), (1, 0), (3, 0), (0, 1))
f32 = jnp.float32
bf16 = jnp.bfloat16


def basis_coefficients(count):
    t = (2.0 * np.arange(count) - (count - 1)) / count
    columns, result = [], []
    for power in range(4):
        vector = t**power
        for prior in columns:
            vector = vector - np.sum(prior * vector) * prior
        vector = vector / np.sqrt(np.sum(vector * vector))
        columns.append(vector)
        powers = list(range(power % 2, power + 1, 2))
        fit = np.linalg.lstsq(np.stack([t**p for p in powers], 1), vector, rcond=None)[0]
        row = [0.0] * 4
        for p, value in zip(powers, fit):
            row[p] = float(value)
        result.append(row)
    return result


def basis_at(coefficients, channel, count):
    t = (2.0 * channel.astype(f32) - (count - 1)) / count
    t2 = t * t
    c = coefficients
    return (
        jnp.full_like(t, c[0][0]),
        c[1][1] * t,
        c[2][2] * t2 + c[2][0],
        (c[3][3] * t2 + c[3][1]) * t,
    )


def two_pieces(x):
    hi = x.astype(bf16)
    return hi, (x - hi.astype(f32)).astype(bf16)


def three_pieces(x):
    hi = x.astype(bf16)
    rest = x - hi.astype(f32)
    mid = rest.astype(bf16)
    return hi, mid, (rest - mid.astype(f32)).astype(bf16)


def pick(one_hot, x):
    return sum(jnp.dot(one_hot, piece, preferred_element_type=f32) for piece in three_pieces(x))


def iota(shape, dim):
    return lax.broadcasted_iota(jnp.int32, shape, dim)


def working_to_given(n):
    pol, row, chan = n // 64, (n // 8) % 8, n % 8
    return chan * 16 + (row // 2) * 4 + pol * 2 + row % 2


def pair_terms(near, far, model, seen_r, seen_i):
    total_r, total_i = -seen_r, -seen_i
    rows = [slice(8 * i, 8 * i + 8) for i in range(8)]
    first = []
    for k in range(SKY_DIRECTIONS):
        re, im = rows[2 * k], rows[2 * k + 1]
        ar, ai, dr, di, cr, ci = near[re], near[im], far[re], far[im], model[re], model[im]
        er = cr * dr + ci * di
        ei = ci * dr - cr * di
        total_r = total_r + (ar * er - ai * ei)
        total_i = total_i + (ar * ei + ai * er)
        first.append((er, ei))
    near_term, far_term = [], []
    for k in range(SKY_DIRECTIONS):
        re, im = rows[2 * k], rows[2 * k + 1]
        ar, ai, cr, ci = near[re], near[im], model[re], model[im]
        er, ei = first[k]
        fr = ar * cr - ai * ci
        fi = ar * ci + ai * cr
        near_term += [total_r * er + total_i * ei, total_i * er - total_r * ei]
        far_term += [total_r * fr + total_i * fi, total_r * fi - total_i * fr]
    return jnp.concatenate(near_term, 0), jnp.concatenate(far_term, 0)


def kernel(
    count,
    coefficients,
    g_hbm, z_hbm, u_hbm, c_hbm, v_hbm, s_hbm,
    g_out, z_out, u_out,
    g_in, z_in, u_in, c_in, v_in, s_in,
    hot, hot_t, model, seen,
    grad, grad_land, half, half_land, gains, part_z, part_x, weights,
    in_sem, rs_s, rs_r, zh_s, zh_r, ag_s, ag_r, pz_s, pz_r, px_s, px_r, aw_s, aw_r,
):
    width = s_in.shape[1]
    stations = g_in.shape[1]
    half_lanes = stations // 2

    chan, bl = lax.axis_index("chan"), lax.axis_index("bl")
    core, z_lo, x = chan % 2, (chan // 2) % 4, chan // 8
    y, z_hi = bl % 8, bl // 8
    zz, xc = z_hi * 4 + z_lo, x * 2 + core

    def y_peer(d):
        return (chan, z_hi * 8 + (y + d) % 8)

    def z_peer(d):
        other = (zz + d) % 8
        return ((x * 4 + other % 4) * 2 + core, (other // 4) * 8 + y)

    def xc_peer(dx, dc):
        return ((((x + dx) % 4) * 4 + z_lo) * 2 + (core + dc) % 2, bl)

    loads = [
        pltpu.make_async_copy(src, dst, in_sem.at[i])
        for i, (src, dst) in enumerate(
            ((s_hbm, s_in), (g_hbm, g_in), (c_hbm, c_in), (v_hbm, v_in), (z_hbm, z_in), (u_hbm, u_in))
        )
    ]
    for load in loads:
        load.start()

    barrier = pltpu.get_barrier_semaphore()
    peers = [y_peer(d) for d in FAR_FIRST] + [z_peer(d) for d in FAR_FIRST] + [xc_peer(*d) for d in XC_FAR_FIRST]
    for peer in peers:
        pl.semaphore_signal(barrier, inc=1, device_id=peer, device_id_type=MESH)

    sent = []

    def send(src, dst, send_sem, recv_sem, peer):
        copy = pltpu.make_async_remote_copy(
            src_ref=src, dst_ref=dst, send_sem=send_sem, recv_sem=recv_sem, device_id=peer, device_id_type=MESH
        )
        copy.start()
        sent.append(copy)
        return copy

    loads[0].wait()
    column = jnp.transpose(s_in[...].astype(f32))
    for end in range(2):
        hot[:, end * width : (end + 1) * width] = jnp.where(
            iota((stations, width), 0) == s_in[end : end + 1, :], 1.0, 0.0
        ).astype(bf16)
        hot_t[end * width : (end + 1) * width, :] = jnp.where(
            iota((width, stations), 1).astype(f32) == column[:, end : end + 1], 1.0, 0.0
        ).astype(bf16)

    turn = jnp.where(working_to_given(iota((128, 128), 0)) == iota((128, 128), 1), 1.0, 0.0).astype(bf16)
    loads[1].wait()
    g_hi, g_lo = (jnp.dot(turn, piece, preferred_element_type=f32).astype(bf16) for piece in two_pieces(g_in[...]))
    loads[2].wait()
    turned = jnp.dot(turn, c_in[...], preferred_element_type=f32)
    for pol in range(2):
        model[pol] = turned[64 * pol : 64 * pol + 64]
    loads[3].wait()
    seen_rows = iota((32, 32), 0)
    seen_turn = jnp.where((seen_rows % 8) * 4 + seen_rows // 8 == iota((32, 32), 1), 1.0, 0.0).astype(bf16)
    turned = pick(seen_turn, v_in[...])
    for row in range(4):
        seen[row] = turned[8 * row : 8 * row + 8]

    def gradient(it, pol):
        if it == 0:
            lhs = jnp.concatenate([g_hi[64 * pol : 64 * pol + 64], g_lo[64 * pol : 64 * pol + 64]], 0)
        else:
            lhs = jnp.concatenate(two_pieces(gains[it - 1, pol].reshape(64, stations)), 0)
        near = jnp.dot(lhs, hot[:, :width], preferred_element_type=f32)
        far = jnp.dot(lhs, hot[:, width:], preferred_element_type=f32)
        near_term, far_term = pair_terms(
            near[:64] + near[64:], far[:64] + far[64:], model[pol], seen[2 * pol], seen[2 * pol + 1]
        )
        total = jnp.dot(jnp.concatenate(two_pieces(near_term), 0), hot_t[:width], preferred_element_type=f32) + jnp.dot(
            jnp.concatenate(two_pieces(far_term), 0), hot_t[width:], preferred_element_type=f32
        )
        grad[it, pol] = (total[:64] + total[64:]).reshape(ROWS, CH, stations)

    def scatter_rows(it, pol):
        return [
            send(
                grad.at[it, pol, (y + d) % 8], grad_land.at[it, pol, i], rs_s.at[it, pol, i], rs_r.at[it, pol, i], y_peer(d)
            )
            for i, d in enumerate(FAR_FIRST)
        ]

    own_basis = basis_at(coefficients, chan * CH + iota((CH, 1), 0), count)
    first_z = jnp.where(z_hi == 0, 1.0, 0.0)

    def take(it, pol, copies, fixed):
        for copy in copies:
            copy.wait_recv()
        total = grad[it, pol, y]
        for i in range(7):
            total = total + grad_land[it, pol, i]
        half[it, pol] = total
        part = first_z * fixed - MU * total
        sums = [jnp.sum(b * part, axis=0, keepdims=True) for b in own_basis]
        part_z[it, pol, zz] = jnp.concatenate(
            [row[:, h * half_lanes : (h + 1) * half_lanes] for h in range(2) for row in sums], 0
        )
        fits = [
            send(part_z.at[it, pol, zz], part_z.at[it, pol, zz], pz_s.at[it, pol, i], pz_r.at[it, pol, i], z_peer(d))
            for i, d in enumerate(FAR_FIRST)
        ]
        pair = send(half.at[it, pol], half_land.at[it, pol], zh_s.at[it, pol], zh_r.at[it, pol], z_peer(4))
        return pair, fits

    def finish(it, pol, pair, base):
        pair.wait_recv()
        new = base - MU * (half[it, pol] + half_land[it, pol])
        gains[it, pol, y] = new
        return new, [
            send(gains.at[it, pol, y], gains.at[it, pol, y], ag_s.at[it, pol, i], ag_r.at[it, pol, i], y_peer(d))
            for i, d in enumerate(FAR_FIRST)
        ]

    def fit_xc(it, pol, copies):
        for copy in copies:
            copy.wait_recv()
        total = part_z[it, pol, 0]
        for i in range(1, 8):
            total = total + part_z[it, pol, i]
        part_x[it, pol, xc] = total
        return [
            send(part_x.at[it, pol, xc], part_x.at[it, pol, xc], px_s.at[it, pol, i], px_r.at[it, pol, i], xc_peer(*d))
            for i, d in enumerate(XC_FAR_FIRST)
        ]

    def spread(it, pol, copies):
        for copy in copies:
            copy.wait_recv()
        total = part_x[it, pol, 0]
        for i in range(1, 8):
            total = total + part_x[it, pol, i]
        weights[it, pol, y] = total
        return total, [
            send(weights.at[it, pol, y], weights.at[it, pol, y], aw_s.at[it, pol, i], aw_r.at[it, pol, i], y_peer(d))
            for i, d in enumerate(FAR_FIRST)
        ]

    def landed(groups):
        for copies in groups:
            for copy in copies:
                copy.wait_recv()

    gradient(0, 0)
    pl.semaphore_wait(barrier, len(peers))
    rows0 = [scatter_rows(0, 0)]
    gradient(0, 1)
    rows0.append(scatter_rows(0, 1))

    loads[4].wait()
    loads[5].wait()
    own_rows = iota((16, 128), 0)
    own_turn = jnp.where(
        (own_rows % 8) * 16 + (y // 2) * 4 + (own_rows // 8) * 2 + y % 2 == iota((16, 128), 1), 1.0, 0.0
    ).astype(bf16)
    kept = g_in[...] - MU * RHO * (g_in[...] - z_in[...] + u_in[...])
    base0, dual0 = pick(own_turn, kept), pick(own_turn, u_in[...])
    base0 = [base0[8 * pol : 8 * pol + 8] for pol in range(2)]
    dual0 = [dual0[8 * pol : 8 * pol + 8] for pol in range(2)]

    took = [take(0, pol, rows0[pol], base0[pol] + dual0[pol]) for pol in range(2)]
    done = [finish(0, pol, took[pol][0], base0[pol]) for pol in range(2)]
    fits = [fit_xc(0, pol, took[pol][1]) for pol in range(2)]

    rows1 = []
    for pol in range(2):
        landed([done[pol][1]])
        gradient(1, pol)
        rows1.append(scatter_rows(1, pol))

    base1, fixed1, spreads = [], [], []
    for pol in range(2):
        weight, copies = spread(0, pol, fits[pol])
        spreads.append(copies)
        fitted = jnp.concatenate(
            [
                sum(own_basis[r] * weight[4 * h + r : 4 * h + r + 1, :] for r in range(4))
                for h in range(2)
            ],
            1,
        )
        new = done[pol][0]
        dual1 = dual0[pol] + new - fitted
        base1.append(new - MU * RHO * (new - fitted + dual1))
        fixed1.append(base1[pol] + dual1)

    back = jnp.where(working_to_given(iota((128, 128), 1)) == iota((128, 128), 0), 1.0, 0.0).astype(bf16)
    given = iota((128, 1), 0)
    given_row = ((given // 2) % 2) * 8 + ((given // 4) % 4) * 2 + given % 2
    values = basis_at(coefficients, chan * CH + given // 16, count)
    slot = iota((1, 128), 1)
    spans = [
        jnp.where(
            (slot // 8 == given_row) & ((slot // 4) % 2 == h),
            sum(jnp.where(slot % 4 == r, values[r], 0.0) for r in range(4)),
            0.0,
        )
        for h in range(2)
    ]

    def evaluate(it):
        flat = weights[it].reshape(128, half_lanes)
        return jnp.concatenate(
            [jnp.dot(span, flat, precision=lax.Precision.HIGHEST, preferred_element_type=f32) for span in spans], 1
        )

    u_out[...] = u_in[...] + pick(back, gains[0].reshape(128, stations))

    took = [take(1, pol, rows1[pol], fixed1[pol]) for pol in range(2)]
    landed(spreads)
    u_out[...] = u_out[...] - evaluate(0)
    fits = [fit_xc(1, pol, took[pol][1]) for pol in range(2)]
    done = [finish(1, pol, took[pol][0], base1[pol]) for pol in range(2)]
    spreads = [spread(1, pol, fits[pol])[1] for pol in range(2)]
    landed([copies for _, copies in done])
    g_new = pick(back, gains[1].reshape(128, stations))
    g_out[...] = g_new
    u_out[...] = u_out[...] + g_new
    landed(spreads)
    fitted = evaluate(1)
    z_out[...] = fitted
    u_out[...] = u_out[...] - fitted
    for copy in sent:
        copy.wait_send()


def body(gains, consensus, dual, coherence, visibility, stations):
    rows, sites = gains.shape
    width = coherence.shape[1]
    count = rows // 16 * lax.axis_size("chan")
    vmem = pltpu.VMEM
    dma = pltpu.SemaphoreType.DMA
    out = jax.ShapeDtypeStruct((rows, sites), f32)
    return pl.pallas_call(
        functools.partial(kernel, count, basis_coefficients(count)),
        out_shape=(out, out, out),
        in_specs=[pl.BlockSpec(memory_space=pl.ANY)] * 6,
        out_specs=tuple([pl.BlockSpec(memory_space=pltpu.VMEM)] * 3),
        scratch_shapes=[
            vmem((rows, sites), f32),
            vmem((rows, sites), f32),
            vmem((rows, sites), f32),
            vmem((rows, width), bf16),
            vmem((rows // 4, width), f32),
            vmem((2, width), jnp.int32),
            vmem((sites, 2 * width), bf16),
            vmem((2 * width, sites), bf16),
            vmem((2, 64, width), f32),
            vmem((4, CH, width), f32),
            vmem((ITERS, 2, ROWS, CH, sites), f32),
            vmem((ITERS, 2, 7, CH, sites), f32),
            vmem((ITERS, 2, CH, sites), f32),
            vmem((ITERS, 2, CH, sites), f32),
            vmem((ITERS, 2, ROWS, CH, sites), f32),
            vmem((ITERS, 2, 8, 8, sites // 2), f32),
            vmem((ITERS, 2, 8, 8, sites // 2), f32),
            vmem((ITERS, 2, 8, 8, sites // 2), f32),
            dma((6,)),
            dma((ITERS, 2, 7)),
            dma((ITERS, 2, 7)),
            dma((ITERS, 2)),
            dma((ITERS, 2)),
            dma((ITERS, 2, 7)),
            dma((ITERS, 2, 7)),
            dma((ITERS, 2, 7)),
            dma((ITERS, 2, 7)),
            dma((ITERS, 2, 7)),
            dma((ITERS, 2, 7)),
            dma((ITERS, 2, 7)),
            dma((ITERS, 2, 7)),
        ],
        compiler_params=pltpu.CompilerParams(collective_id=0, has_side_effects=True, vmem_limit_bytes=62 << 20),
    )(gains, consensus, dual, coherence, visibility, stations)


def solution(mesh):
    in_specs = (
        P("chan", None),
        P("chan", None),
        P("chan", None),
        P("chan", "bl"),
        P("chan", "bl"),
        P(None, "bl"),
    )
    out_specs = (P("chan", None), P("chan", None), P("chan", None))
    return jax.shard_map(body, mesh=mesh, in_specs=in_specs, out_specs=out_specs, check_vma=False)
```

```python
import functools

import jax
import jax.numpy as jnp
import numpy as np
from jax import lax
from jax.experimental import pallas as pl
from jax.experimental.pallas import tpu as pltpu
from jax.sharding import PartitionSpec as P

SKY_DIRECTIONS = 4
ITERS = 2
MU = 0.02
RHO = 25.0

CH = 8
SPAN = 256
ROWS = 8
MESH = pl.DeviceIdType.MESH
FAR_FIRST = (4, 3, 5, 2, 6, 1, 7)
XC_FAR_FIRST = ((2, 1), (2, 0), (1, 1), (3, 1), (1, 0), (3, 0), (0, 1))
f32 = jnp.float32
bf16 = jnp.bfloat16


def basis_coefficients(count):
    t = (2.0 * np.arange(count) - (count - 1)) / count
    columns, result = [], []
    for power in range(4):
        vector = t**power
        for prior in columns:
            vector = vector - np.sum(prior * vector) * prior
        vector = vector / np.sqrt(np.sum(vector * vector))
        columns.append(vector)
        powers = list(range(power % 2, power + 1, 2))
        fit = np.linalg.lstsq(np.stack([t**p for p in powers], 1), vector, rcond=None)[0]
        row = [0.0] * 4
        for p, value in zip(powers, fit):
            row[p] = float(value)
        result.append(row)
    return result


def basis_at(coefficients, channel, count):
    t = (2.0 * channel.astype(f32) - (count - 1)) / count
    t2 = t * t
    c = coefficients
    return (
        jnp.full_like(t, c[0][0]),
        c[1][1] * t,
        c[2][2] * t2 + c[2][0],
        (c[3][3] * t2 + c[3][1]) * t,
    )


def two_pieces(x):
    hi = x.astype(bf16)
    return hi, (x - hi.astype(f32)).astype(bf16)


def three_pieces(x):
    hi = x.astype(bf16)
    rest = x - hi.astype(f32)
    mid = rest.astype(bf16)
    return hi, mid, (rest - mid.astype(f32)).astype(bf16)


def pick(one_hot, x):
    return sum(jnp.dot(one_hot, piece, preferred_element_type=f32) for piece in three_pieces(x))


def iota(shape, dim):
    return lax.broadcasted_iota(jnp.int32, shape, dim)


def working_to_given(n):
    pol, row, chan = n // 64, (n // 8) % 8, n % 8
    return chan * 16 + (row // 2) * 4 + pol * 2 + row % 2


def pair_terms(near, far, model, seen_r, seen_i):
    total_r, total_i = -seen_r, -seen_i
    rows = [slice(8 * i, 8 * i + 8) for i in range(8)]
    first = []
    for k in range(SKY_DIRECTIONS):
        re, im = rows[2 * k], rows[2 * k + 1]
        ar, ai, dr, di, cr, ci = near[re], near[im], far[re], far[im], model[re], model[im]
        er = cr * dr + ci * di
        ei = ci * dr - cr * di
        total_r = total_r + (ar * er - ai * ei)
        total_i = total_i + (ar * ei + ai * er)
        first.append((er, ei))
    near_term, far_term = [], []
    for k in range(SKY_DIRECTIONS):
        re, im = rows[2 * k], rows[2 * k + 1]
        ar, ai, cr, ci = near[re], near[im], model[re], model[im]
        er, ei = first[k]
        fr = ar * cr - ai * ci
        fi = ar * ci + ai * cr
        near_term += [total_r * er + total_i * ei, total_i * er - total_r * ei]
        far_term += [total_r * fr + total_i * fi, total_r * fi - total_i * fr]
    return jnp.concatenate(near_term, 0), jnp.concatenate(far_term, 0)


def kernel(
    count,
    coefficients,
    g_hbm, z_hbm, u_hbm, c_hbm, v_hbm, s_hbm,
    g_out, z_out, u_out,
    g_in, z_in, u_in, c_in, v_in, s_in,
    hot, hot_t, model, seen,
    grad, grad_land, half, half_land, gains, part_z, part_x, weights,
    in_sem, rs_s, rs_r, zh_s, zh_r, ag_s, ag_r, pz_s, pz_r, px_s, px_r, aw_s, aw_r,
):
    width = s_in.shape[1]
    stations = g_in.shape[1]

    chan, bl = lax.axis_index("chan"), lax.axis_index("bl")
    core, z_lo, x = chan % 2, (chan // 2) % 4, chan // 8
    y, z_hi = bl % 8, bl // 8
    zz, xc = z_hi * 4 + z_lo, x * 2 + core

    def y_peer(d):
        return (chan, z_hi * 8 + (y + d) % 8)

    def z_peer(d):
        other = (zz + d) % 8
        return ((x * 4 + other % 4) * 2 + core, (other // 4) * 8 + y)

    def xc_peer(dx, dc):
        return ((((x + dx) % 4) * 4 + z_lo) * 2 + (core + dc) % 2, bl)

    loads = [
        pltpu.make_async_copy(src, dst, in_sem.at[i])
        for i, (src, dst) in enumerate(
            ((s_hbm, s_in), (g_hbm, g_in), (c_hbm, c_in), (v_hbm, v_in), (z_hbm, z_in), (u_hbm, u_in))
        )
    ]
    for load in loads:
        load.start()

    barrier = pltpu.get_barrier_semaphore()
    peers = [y_peer(d) for d in FAR_FIRST] + [z_peer(d) for d in FAR_FIRST] + [xc_peer(*d) for d in XC_FAR_FIRST]
    for peer in peers:
        pl.semaphore_signal(barrier, inc=1, device_id=peer, device_id_type=MESH)

    sent = []

    def send(src, dst, send_sem, recv_sem, peer):
        copy = pltpu.make_async_remote_copy(
            src_ref=src, dst_ref=dst, send_sem=send_sem, recv_sem=recv_sem, device_id=peer, device_id_type=MESH
        )
        copy.start()
        sent.append(copy)
        return copy

    loads[0].wait()
    column = jnp.transpose(s_in[...].astype(f32))
    for end in range(2):
        ids = s_in[end : end + 1, :]
        for low in range(0, stations, SPAN):
            local = jnp.where((ids >= low) & (ids < low + SPAN), ids - low, -1).astype(f32).astype(bf16)
            hot[low : low + SPAN, end * width : (end + 1) * width] = jnp.where(
                iota((SPAN, 1), 0).astype(f32).astype(bf16) == local, jnp.ones((), bf16), jnp.zeros((), bf16)
            )
        hot_t[end * width : (end + 1) * width, :] = jnp.where(
            iota((width, stations), 1).astype(f32) == column[:, end : end + 1], 1.0, 0.0
        ).astype(bf16)

    turn = jnp.where(working_to_given(iota((128, 128), 0)) == iota((128, 128), 1), 1.0, 0.0).astype(bf16)
    loads[1].wait()
    g_hi, g_lo = (jnp.dot(turn, piece, preferred_element_type=f32).astype(bf16) for piece in two_pieces(g_in[...]))
    loads[2].wait()
    turned = jnp.dot(turn, c_in[...], preferred_element_type=f32)
    for pol in range(2):
        model[pol] = turned[64 * pol : 64 * pol + 64]
    loads[3].wait()
    seen_rows = iota((32, 32), 0)
    seen_turn = jnp.where((seen_rows % 8) * 4 + seen_rows // 8 == iota((32, 32), 1), 1.0, 0.0).astype(bf16)
    turned = pick(seen_turn, v_in[...])
    for row in range(4):
        seen[row] = turned[8 * row : 8 * row + 8]

    def gradient(it, pol):
        if it == 0:
            lhs = jnp.concatenate([g_hi[64 * pol : 64 * pol + 64], g_lo[64 * pol : 64 * pol + 64]], 0)
        else:
            lhs = jnp.concatenate(two_pieces(gains[it - 1, pol].reshape(64, stations)), 0)
        near = jnp.dot(lhs, hot[:, :width], preferred_element_type=f32)
        far = jnp.dot(lhs, hot[:, width:], preferred_element_type=f32)
        near_term, far_term = pair_terms(
            near[:64] + near[64:], far[:64] + far[64:], model[pol], seen[2 * pol], seen[2 * pol + 1]
        )
        total = jnp.dot(jnp.concatenate(two_pieces(near_term), 0), hot_t[:width], preferred_element_type=f32) + jnp.dot(
            jnp.concatenate(two_pieces(far_term), 0), hot_t[width:], preferred_element_type=f32
        )
        grad[it, pol] = (total[:64] + total[64:]).reshape(ROWS, CH, stations)

    def scatter_rows(it, pol):
        return [
            send(
                grad.at[it, pol, (y + d) % 8], grad_land.at[it, pol, i], rs_s.at[it, pol, i], rs_r.at[it, pol, i], y_peer(d)
            )
            for i, d in enumerate(FAR_FIRST)
        ]

    own_basis = basis_at(coefficients, chan * CH + iota((CH, 1), 0), count)
    first_z = jnp.where(z_hi == 0, 1.0, 0.0)

    def take(it, pol, copies):
        arrived(copies)
        total = grad[it, pol, y]
        for i in range(7):
            total = total + grad_land[it, pol, i]
        half[it, pol] = total
        return total

    def pair(it, pol):
        return send(half.at[it, pol], half_land.at[it, pol], zh_s.at[it, pol], zh_r.at[it, pol], z_peer(4))

    def finish(it, pol, copy, base):
        copy.wait_recv()
        new = base - MU * (half[it, pol] + half_land[it, pol])
        gains[it, pol, y] = new
        return new, [
            send(gains.at[it, pol, y], gains.at[it, pol, y], ag_s.at[it, pol, i], ag_r.at[it, pol, i], y_peer(d))
            for i, d in enumerate(FAR_FIRST)
        ]

    def coefficient_rows(pol, part):
        row = iota((8, stations), 0)
        result = jnp.zeros((8, stations), f32)
        for r, b in enumerate(own_basis):
            result = jnp.where(row == 4 * pol + r, jnp.sum(b * part, axis=0, keepdims=True), result)
        return result

    def fit_z(it, coefficient):
        part_z[it, zz] = coefficient
        return [
            send(part_z.at[it, zz], part_z.at[it, zz], pz_s.at[it, i], pz_r.at[it, i], z_peer(d))
            for i, d in enumerate(FAR_FIRST)
        ]

    def fit_xc(it, copies):
        arrived(copies)
        part_x[it, xc] = total_of(part_z, it)
        return [
            send(part_x.at[it, xc], part_x.at[it, xc], px_s.at[it, i], px_r.at[it, i], xc_peer(*d))
            for i, d in enumerate(XC_FAR_FIRST)
        ]

    def fit_done(it, copies):
        arrived(copies)
        total = total_of(part_x, it)
        weights[it, y] = total
        return total

    def spread(it):
        return [
            send(weights.at[it, y], weights.at[it, y], aw_s.at[it, i], aw_r.at[it, i], y_peer(d))
            for i, d in enumerate(FAR_FIRST)
        ]

    def total_of(parts, it):
        total = parts[it, 0]
        for i in range(1, 8):
            total = total + parts[it, i]
        return total

    def arrived(copies):
        for copy in copies:
            copy.wait_recv()

    gradient(0, 0)
    pl.semaphore_wait(barrier, len(peers))
    rows0 = [scatter_rows(0, 0)]
    gradient(0, 1)
    rows0.append(scatter_rows(0, 1))

    loads[4].wait()
    loads[5].wait()
    own_rows = iota((16, 128), 0)
    own_turn = jnp.where(
        (own_rows % 8) * 16 + (y // 2) * 4 + (own_rows // 8) * 2 + y % 2 == iota((16, 128), 1), 1.0, 0.0
    ).astype(bf16)
    kept = g_in[...] - MU * RHO * (g_in[...] - z_in[...] + u_in[...])
    base0, dual0 = pick(own_turn, kept), pick(own_turn, u_in[...])
    base0 = [base0[8 * pol : 8 * pol + 8] for pol in range(2)]
    dual0 = [dual0[8 * pol : 8 * pol + 8] for pol in range(2)]

    pairs = []
    totals = [take(0, 0, rows0[0])]
    pairs.append(pair(0, 0))
    totals.append(take(0, 1, rows0[1]))
    pairs.append(pair(0, 1))
    fits = fit_z(
        0, sum(coefficient_rows(pol, first_z * (base0[pol] + dual0[pol]) - MU * totals[pol]) for pol in range(2))
    )
    done = [finish(0, 0, pairs[0], base0[0])]
    done.append(finish(0, 1, pairs[1], base0[1]))

    arrived(done[0][1])
    gradient(1, 0)
    rows1 = [scatter_rows(1, 0)]
    fits = fit_xc(0, fits)
    arrived(done[1][1])
    gradient(1, 1)
    rows1.append(scatter_rows(1, 1))

    weight = fit_done(0, fits)
    base1, fixed1 = [], []
    for pol in range(2):
        fitted = sum(own_basis[r] * weight[4 * pol + r : 4 * pol + r + 1, :] for r in range(4))
        new = done[pol][0]
        dual1 = dual0[pol] + new - fitted
        base1.append(new - MU * RHO * (new - fitted + dual1))
        fixed1.append(first_z * (base1[pol] + dual1))

    back = jnp.where(working_to_given(iota((128, 128), 1)) == iota((128, 128), 0), 1.0, 0.0).astype(bf16)
    given = iota((128, 1), 0)
    given_row = (((given // 4) % 4) * 2 + given % 2) * 2 + (given // 2) % 2
    values = basis_at(coefficients, chan * CH + given // 16, count)
    slot = iota((1, 64), 1)
    span = jnp.where(
        slot // 4 == given_row, sum(jnp.where(slot % 4 == r, values[r], 0.0) for r in range(4)), 0.0
    )

    def evaluate(it):
        flat = weights[it].reshape(64, stations)
        return jnp.dot(span, flat, precision=lax.Precision.HIGHEST, preferred_element_type=f32)

    u_out[...] = u_in[...] + pick(back, gains[0].reshape(128, stations))

    total = take(1, 0, rows1[0])
    pairs = [pair(1, 0)]
    coefficient = coefficient_rows(0, fixed1[0] - MU * total)
    total = take(1, 1, rows1[1])
    fits = fit_z(1, coefficient + coefficient_rows(1, fixed1[1] - MU * total))
    pairs.append(pair(1, 1))
    spreads = spread(0)
    done = [finish(1, 0, pairs[0], base1[0])[1]]
    fits = fit_xc(1, fits)
    done.append(finish(1, 1, pairs[1], base1[1])[1])
    arrived(spreads)
    u_out[...] = u_out[...] - evaluate(0)
    fit_done(1, fits)
    spreads = spread(1)
    for copies in done:
        arrived(copies)
    g_new = pick(back, gains[1].reshape(128, stations))
    g_out[...] = g_new
    u_out[...] = u_out[...] + g_new
    arrived(spreads)
    fitted = evaluate(1)
    z_out[...] = fitted
    u_out[...] = u_out[...] - fitted
    for copy in sent:
        copy.wait_send()


def store(*refs):
    n = len(refs) // 2
    copies = [pltpu.make_async_copy(refs[i], refs[n + i], refs[-1].at[i]) for i in range(n)]
    for copy in copies:
        copy.start()
    for copy in copies:
        copy.wait()


def body(gains, consensus, dual, coherence, visibility, stations):
    rows, sites = gains.shape
    width = coherence.shape[1]
    count = rows // 16 * lax.axis_size("chan")
    vmem = pltpu.VMEM
    dma = pltpu.SemaphoreType.DMA
    out = jax.ShapeDtypeStruct((rows, sites), f32)
    results = pl.pallas_call(
        functools.partial(kernel, count, basis_coefficients(count)),
        out_shape=(pltpu.VMEM((rows, sites), f32),) * 3,
        in_specs=[pl.BlockSpec(memory_space=pltpu.HBM)] * 6,
        out_specs=tuple([pl.BlockSpec(memory_space=pltpu.VMEM)] * 3),
        scratch_shapes=[
            vmem((rows, sites), f32),
            vmem((rows, sites), f32),
            vmem((rows, sites), f32),
            vmem((rows, width), bf16),
            vmem((rows // 4, width), f32),
            vmem((2, width), jnp.int32),
            vmem((sites, 2 * width), bf16),
            vmem((2 * width, sites), bf16),
            vmem((2, 64, width), f32),
            vmem((4, CH, width), f32),
            vmem((ITERS, 2, ROWS, CH, sites), f32),
            vmem((ITERS, 2, 7, CH, sites), f32),
            vmem((ITERS, 2, CH, sites), f32),
            vmem((ITERS, 2, CH, sites), f32),
            vmem((ITERS, 2, ROWS, CH, sites), f32),
            vmem((ITERS, 8, 8, sites), f32),
            vmem((ITERS, 8, 8, sites), f32),
            vmem((ITERS, 8, 8, sites), f32),
            dma((6,)),
            dma((ITERS, 2, 7)),
            dma((ITERS, 2, 7)),
            dma((ITERS, 2)),
            dma((ITERS, 2)),
            dma((ITERS, 2, 7)),
            dma((ITERS, 2, 7)),
            dma((ITERS, 7)),
            dma((ITERS, 7)),
            dma((ITERS, 7)),
            dma((ITERS, 7)),
            dma((ITERS, 7)),
            dma((ITERS, 7)),
        ],
        compiler_params=pltpu.CompilerParams(collective_id=0, has_side_effects=True, vmem_limit_bytes=44 << 20),
    )(*(pltpu.with_memory_space_constraint(x, pltpu.HBM) for x in (gains, consensus, dual, coherence, visibility, stations)))
    return pl.pallas_call(
        store,
        out_shape=(out, out, out),
        in_specs=[pl.BlockSpec(memory_space=pltpu.VMEM)] * 3,
        out_specs=tuple([pl.BlockSpec(memory_space=pl.ANY)] * 3),
        scratch_shapes=[dma((3,))],
    )(*(pltpu.with_memory_space_constraint(x, pltpu.VMEM) for x in results))


def solution(mesh):
    in_specs = (
        P("chan", None),
        P("chan", None),
        P("chan", None),
        P("chan", "bl"),
        P("chan", "bl"),
        P(None, "bl"),
    )
    out_specs = (P("chan", None), P("chan", None), P("chan", None))
    return jax.shard_map(body, mesh=mesh, in_specs=in_specs, out_specs=out_specs, check_vma=False)
```

```python
import functools

import jax
import jax.numpy as jnp
import numpy as np
from jax import lax
from jax.experimental import pallas as pl
from jax.experimental.pallas import tpu as pltpu
from jax.sharding import PartitionSpec as P

SKY_DIRECTIONS = 4
ITERS = 2
MU = 0.02
RHO = 25.0

CH = 8
SPAN = 256
ROWS = 8
MESH = pl.DeviceIdType.MESH
FAR_FIRST = (4, 3, 5, 2, 6, 1, 7)
XC_FAR_FIRST = ((2, 1), (2, 0), (1, 1), (3, 1), (1, 0), (3, 0), (0, 1))
f32 = jnp.float32
bf16 = jnp.bfloat16


def basis_coefficients(count):
    t = (2.0 * np.arange(count) - (count - 1)) / count
    columns, result = [], []
    for power in range(4):
        vector = t**power
        for prior in columns:
            vector = vector - np.sum(prior * vector) * prior
        vector = vector / np.sqrt(np.sum(vector * vector))
        columns.append(vector)
        powers = list(range(power % 2, power + 1, 2))
        fit = np.linalg.lstsq(np.stack([t**p for p in powers], 1), vector, rcond=None)[0]
        row = [0.0] * 4
        for p, value in zip(powers, fit):
            row[p] = float(value)
        result.append(row)
    return result


def basis_at(coefficients, channel, count):
    t = (2.0 * channel.astype(f32) - (count - 1)) / count
    t2 = t * t
    c = coefficients
    return (
        jnp.full_like(t, c[0][0]),
        c[1][1] * t,
        c[2][2] * t2 + c[2][0],
        (c[3][3] * t2 + c[3][1]) * t,
    )


def two_pieces(x):
    hi = x.astype(bf16)
    return hi, (x - hi.astype(f32)).astype(bf16)


def three_pieces(x):
    hi = x.astype(bf16)
    rest = x - hi.astype(f32)
    mid = rest.astype(bf16)
    return hi, mid, (rest - mid.astype(f32)).astype(bf16)


def pick(one_hot, x):
    return sum(jnp.dot(one_hot, piece, preferred_element_type=f32) for piece in three_pieces(x))


def iota(shape, dim):
    return lax.broadcasted_iota(jnp.int32, shape, dim)


def working_to_given(n):
    pol, row, chan = n // 64, (n // 8) % 8, n % 8
    return chan * 16 + (row // 2) * 4 + pol * 2 + row % 2


def pair_terms(near, far, model, seen_r, seen_i):
    total_r, total_i = -seen_r, -seen_i
    rows = [slice(8 * i, 8 * i + 8) for i in range(8)]
    first = []
    for k in range(SKY_DIRECTIONS):
        re, im = rows[2 * k], rows[2 * k + 1]
        ar, ai, dr, di, cr, ci = near[re], near[im], far[re], far[im], model[re], model[im]
        er = cr * dr + ci * di
        ei = ci * dr - cr * di
        total_r = total_r + (ar * er - ai * ei)
        total_i = total_i + (ar * ei + ai * er)
        first.append((er, ei))
    near_term, far_term = [], []
    for k in range(SKY_DIRECTIONS):
        re, im = rows[2 * k], rows[2 * k + 1]
        ar, ai, cr, ci = near[re], near[im], model[re], model[im]
        er, ei = first[k]
        fr = ar * cr - ai * ci
        fi = ar * ci + ai * cr
        near_term += [total_r * er + total_i * ei, total_i * er - total_r * ei]
        far_term += [total_r * fr + total_i * fi, total_r * fi - total_i * fr]
    return jnp.concatenate(near_term, 0), jnp.concatenate(far_term, 0)


def kernel(
    count,
    coefficients,
    g_hbm, z_hbm, u_hbm, c_hbm, v_hbm, s_hbm,
    g_out, z_out, u_out,
    g_in, z_in, u_in, c_in, v_in, s_in,
    hot, hot_t, model, seen,
    grad, grad_land, half, half_land, gains, part_z, part_x, weights,
    in_sem, rs_s, rs_r, zh_s, zh_r, ag_s, ag_r, pz_s, pz_r, px_s, px_r, aw_s, aw_r,
):
    width = s_in.shape[1]
    stations = g_in.shape[1]

    chan, bl = lax.axis_index("chan"), lax.axis_index("bl")
    core, z_lo, x = chan % 2, (chan // 2) % 4, chan // 8
    y, z_hi = bl % 8, bl // 8
    zz, xc = z_hi * 4 + z_lo, x * 2 + core

    def y_peer(d):
        return (chan, z_hi * 8 + (y + d) % 8)

    def z_peer(d):
        other = (zz + d) % 8
        return ((x * 4 + other % 4) * 2 + core, (other // 4) * 8 + y)

    def xc_peer(dx, dc):
        return ((((x + dx) % 4) * 4 + z_lo) * 2 + (core + dc) % 2, bl)

    loads = [
        pltpu.make_async_copy(src, dst, in_sem.at[i])
        for i, (src, dst) in enumerate(
            ((s_hbm, s_in), (g_hbm, g_in), (c_hbm, c_in), (v_hbm, v_in), (z_hbm, z_in), (u_hbm, u_in))
        )
    ]
    for load in loads:
        load.start()

    barrier = pltpu.get_barrier_semaphore()
    peers = [y_peer(d) for d in FAR_FIRST] + [z_peer(d) for d in FAR_FIRST] + [xc_peer(*d) for d in XC_FAR_FIRST]
    for peer in peers:
        pl.semaphore_signal(barrier, inc=1, device_id=peer, device_id_type=MESH)

    sent = []

    def send(src, dst, send_sem, recv_sem, peer):
        copy = pltpu.make_async_remote_copy(
            src_ref=src, dst_ref=dst, send_sem=send_sem, recv_sem=recv_sem, device_id=peer, device_id_type=MESH
        )
        copy.start()
        sent.append(copy)
        return copy

    loads[0].wait()
    for end in range(2):
        ids = s_in[end : end + 1, :]
        for low in range(0, stations, SPAN):
            local = jnp.where((ids >= low) & (ids < low + SPAN), ids - low, -1).astype(f32).astype(bf16)
            hot[low : low + SPAN, end * width : (end + 1) * width] = jnp.where(
                iota((SPAN, 1), 0).astype(f32).astype(bf16) == local, jnp.ones((), bf16), jnp.zeros((), bf16)
            )
    for load in loads[1:4]:
        load.wait()
    column = jnp.transpose(s_in[...].astype(f32))
    for end in range(2):
        for low in range(0, stations, SPAN):
            local = column[:, end : end + 1] - low
            local = jnp.where((local >= 0.0) & (local < SPAN), local, -1.0)
            local = jnp.broadcast_to(local, (width, 128)).astype(bf16)
            for lane in range(0, SPAN, 128):
                hot_t[end * width : (end + 1) * width, low + lane : low + lane + 128] = jnp.where(
                    (iota((1, 128), 1) + lane).astype(f32).astype(bf16) == local, jnp.ones((), bf16), jnp.zeros((), bf16)
                )

    turn = jnp.where(working_to_given(iota((128, 128), 0)) == iota((128, 128), 1), 1.0, 0.0).astype(bf16)
    g_hi, g_lo = (jnp.dot(turn, piece, preferred_element_type=f32).astype(bf16) for piece in two_pieces(g_in[...]))
    turned = jnp.dot(turn, c_in[...], preferred_element_type=f32)
    for pol in range(2):
        model[pol] = turned[64 * pol : 64 * pol + 64]
    seen_rows = iota((32, 32), 0)
    seen_turn = jnp.where((seen_rows % 8) * 4 + seen_rows // 8 == iota((32, 32), 1), 1.0, 0.0).astype(bf16)
    turned = pick(seen_turn, v_in[...])
    for row in range(4):
        seen[row] = turned[8 * row : 8 * row + 8]

    def gradient(it, pol):
        if it == 0:
            lhs = jnp.concatenate([g_hi[64 * pol : 64 * pol + 64], g_lo[64 * pol : 64 * pol + 64]], 0)
        else:
            lhs = jnp.concatenate(two_pieces(gains[it - 1, pol].reshape(64, stations)), 0)
        near = jnp.dot(lhs, hot[:, :width], preferred_element_type=f32)
        far = jnp.dot(lhs, hot[:, width:], preferred_element_type=f32)
        near_term, far_term = pair_terms(
            near[:64] + near[64:], far[:64] + far[64:], model[pol], seen[2 * pol], seen[2 * pol + 1]
        )
        total = jnp.dot(jnp.concatenate(two_pieces(near_term), 0), hot_t[:width], preferred_element_type=f32) + jnp.dot(
            jnp.concatenate(two_pieces(far_term), 0), hot_t[width:], preferred_element_type=f32
        )
        grad[it, pol] = (total[:64] + total[64:]).reshape(ROWS, CH, stations)

    def scatter_rows(it, pol):
        return [
            send(
                grad.at[it, pol, (y + d) % 8], grad_land.at[it, pol, i], rs_s.at[it, pol, i], rs_r.at[it, pol, i], y_peer(d)
            )
            for i, d in enumerate(FAR_FIRST)
        ]

    own_basis = basis_at(coefficients, chan * CH + iota((CH, 1), 0), count)
    first_z = jnp.where(z_hi == 0, 1.0, 0.0)

    def take(it, pol, copies):
        arrived(copies)
        total = grad[it, pol, y]
        for i in range(7):
            total = total + grad_land[it, pol, i]
        half[it, pol] = total
        return total

    def pair(it, pol):
        return send(half.at[it, pol], half_land.at[it, pol], zh_s.at[it, pol], zh_r.at[it, pol], z_peer(4))

    def finish(it, pol, copy, base):
        copy.wait_recv()
        new = base - MU * (half[it, pol] + half_land[it, pol])
        gains[it, pol, y] = new
        return new, [
            send(gains.at[it, pol, y], gains.at[it, pol, y], ag_s.at[it, pol, i], ag_r.at[it, pol, i], y_peer(d))
            for i, d in enumerate(FAR_FIRST)
        ]

    def coefficient_rows(pol, part):
        row = iota((8, stations), 0)
        result = jnp.zeros((8, stations), f32)
        for r, b in enumerate(own_basis):
            result = jnp.where(row == 4 * pol + r, jnp.sum(b * part, axis=0, keepdims=True), result)
        return result

    def fit_z(it, coefficient):
        part_z[it, zz] = coefficient
        return [
            send(part_z.at[it, zz], part_z.at[it, zz], pz_s.at[it, i], pz_r.at[it, i], z_peer(d))
            for i, d in enumerate(FAR_FIRST)
        ]

    def fit_xc(it, copies):
        arrived(copies)
        part_x[it, xc] = total_of(part_z, it)
        return [
            send(part_x.at[it, xc], part_x.at[it, xc], px_s.at[it, i], px_r.at[it, i], xc_peer(*d))
            for i, d in enumerate(XC_FAR_FIRST)
        ]

    def fit_done(it, copies):
        arrived(copies)
        total = total_of(part_x, it)
        weights[it, y] = total
        return total

    def spread(it):
        return [
            send(weights.at[it, y], weights.at[it, y], aw_s.at[it, i], aw_r.at[it, i], y_peer(d))
            for i, d in enumerate(FAR_FIRST)
        ]

    def total_of(parts, it):
        total = parts[it, 0]
        for i in range(1, 8):
            total = total + parts[it, i]
        return total

    def arrived(copies):
        for copy in copies:
            copy.wait_recv()

    gradient(0, 0)
    pl.semaphore_wait(barrier, len(peers))
    rows0 = [scatter_rows(0, 0)]
    gradient(0, 1)
    rows0.append(scatter_rows(0, 1))

    loads[4].wait()
    loads[5].wait()
    own_rows = iota((16, 128), 0)
    own_turn = jnp.where(
        (own_rows % 8) * 16 + (y // 2) * 4 + (own_rows // 8) * 2 + y % 2 == iota((16, 128), 1), 1.0, 0.0
    ).astype(bf16)
    kept = g_in[...] - MU * RHO * (g_in[...] - z_in[...] + u_in[...])
    base0, dual0 = pick(own_turn, kept), pick(own_turn, u_in[...])
    base0 = [base0[8 * pol : 8 * pol + 8] for pol in range(2)]
    dual0 = [dual0[8 * pol : 8 * pol + 8] for pol in range(2)]

    pairs = []
    totals = [take(0, 0, rows0[0])]
    pairs.append(pair(0, 0))
    totals.append(take(0, 1, rows0[1]))
    pairs.append(pair(0, 1))
    fits = fit_z(
        0, sum(coefficient_rows(pol, first_z * (base0[pol] + dual0[pol]) - MU * totals[pol]) for pol in range(2))
    )
    done = [finish(0, 0, pairs[0], base0[0])]
    done.append(finish(0, 1, pairs[1], base0[1]))

    arrived(done[0][1])
    gradient(1, 0)
    rows1 = [scatter_rows(1, 0)]
    fits = fit_xc(0, fits)
    arrived(done[1][1])
    gradient(1, 1)
    rows1.append(scatter_rows(1, 1))

    weight = fit_done(0, fits)
    base1, fixed1 = [], []
    for pol in range(2):
        fitted = sum(own_basis[r] * weight[4 * pol + r : 4 * pol + r + 1, :] for r in range(4))
        new = done[pol][0]
        dual1 = dual0[pol] + new - fitted
        base1.append(new - MU * RHO * (new - fitted + dual1))
        fixed1.append(first_z * (base1[pol] + dual1))

    back = jnp.where(working_to_given(iota((128, 128), 1)) == iota((128, 128), 0), 1.0, 0.0).astype(bf16)
    given = iota((128, 1), 0)
    given_row = (((given // 4) % 4) * 2 + given % 2) * 2 + (given // 2) % 2
    values = basis_at(coefficients, chan * CH + given // 16, count)
    slot = iota((1, 64), 1)
    span = jnp.where(
        slot // 4 == given_row, sum(jnp.where(slot % 4 == r, values[r], 0.0) for r in range(4)), 0.0
    )

    span_hi, span_lo = two_pieces(span)
    spans = jnp.concatenate([span_hi, span_hi, span_lo, span_lo], 1)

    def evaluate(it):
        hi, lo = two_pieces(weights[it].reshape(64, stations))
        return jnp.dot(spans, jnp.concatenate([hi, lo, hi, lo], 0), preferred_element_type=f32)

    u_out[...] = u_in[...] + pick(back, gains[0].reshape(128, stations))

    total = take(1, 0, rows1[0])
    pairs = [pair(1, 0)]
    coefficient = coefficient_rows(0, fixed1[0] - MU * total)
    total = take(1, 1, rows1[1])
    fits = fit_z(1, coefficient + coefficient_rows(1, fixed1[1] - MU * total))
    pairs.append(pair(1, 1))
    spreads = spread(0)
    done = [finish(1, 0, pairs[0], base1[0])[1]]
    fits = fit_xc(1, fits)
    done.append(finish(1, 1, pairs[1], base1[1])[1])
    arrived(spreads)
    u_out[...] = u_out[...] - evaluate(0)
    fit_done(1, fits)
    spreads = spread(1)
    for copies in done:
        arrived(copies)
    g_new = pick(back, gains[1].reshape(128, stations))
    g_out[...] = g_new
    u_out[...] = u_out[...] + g_new
    arrived(spreads)
    fitted = evaluate(1)
    z_out[...] = fitted
    u_out[...] = u_out[...] - fitted
    for copy in sent:
        copy.wait_send()


def store(*refs):
    n = len(refs) // 2
    copies = [pltpu.make_async_copy(refs[i], refs[n + i], refs[-1].at[i]) for i in range(n)]
    for copy in copies:
        copy.start()
    for copy in copies:
        copy.wait()


def body(gains, consensus, dual, coherence, visibility, stations):
    rows, sites = gains.shape
    width = coherence.shape[1]
    count = rows // 16 * lax.axis_size("chan")
    vmem = pltpu.VMEM
    dma = pltpu.SemaphoreType.DMA
    out = jax.ShapeDtypeStruct((rows, sites), f32)
    results = pl.pallas_call(
        functools.partial(kernel, count, basis_coefficients(count)),
        out_shape=(pltpu.VMEM((rows, sites), f32),) * 3,
        in_specs=[pl.BlockSpec(memory_space=pltpu.HBM)] * 6,
        out_specs=tuple([pl.BlockSpec(memory_space=pltpu.VMEM)] * 3),
        scratch_shapes=[
            vmem((rows, sites), f32),
            vmem((rows, sites), f32),
            vmem((rows, sites), f32),
            vmem((rows, width), bf16),
            vmem((rows // 4, width), f32),
            vmem((2, width), jnp.int32),
            vmem((sites, 2 * width), bf16),
            vmem((2 * width, sites), bf16),
            vmem((2, 64, width), f32),
            vmem((4, CH, width), f32),
            vmem((ITERS, 2, ROWS, CH, sites), f32),
            vmem((ITERS, 2, 7, CH, sites), f32),
            vmem((ITERS, 2, CH, sites), f32),
            vmem((ITERS, 2, CH, sites), f32),
            vmem((ITERS, 2, ROWS, CH, sites), f32),
            vmem((ITERS, 8, 8, sites), f32),
            vmem((ITERS, 8, 8, sites), f32),
            vmem((ITERS, 8, 8, sites), f32),
            dma((6,)),
            dma((ITERS, 2, 7)),
            dma((ITERS, 2, 7)),
            dma((ITERS, 2)),
            dma((ITERS, 2)),
            dma((ITERS, 2, 7)),
            dma((ITERS, 2, 7)),
            dma((ITERS, 7)),
            dma((ITERS, 7)),
            dma((ITERS, 7)),
            dma((ITERS, 7)),
            dma((ITERS, 7)),
            dma((ITERS, 7)),
        ],
        compiler_params=pltpu.CompilerParams(collective_id=0, has_side_effects=True, vmem_limit_bytes=44 << 20),
    )(*(pltpu.with_memory_space_constraint(x, pltpu.HBM) for x in (gains, consensus, dual, coherence, visibility, stations)))
    return pl.pallas_call(
        store,
        out_shape=(out, out, out),
        in_specs=[pl.BlockSpec(memory_space=pltpu.VMEM)] * 3,
        out_specs=tuple([pl.BlockSpec(memory_space=pl.ANY)] * 3),
        scratch_shapes=[dma((3,))],
    )(*(pltpu.with_memory_space_constraint(x, pltpu.VMEM) for x in results))


def solution(mesh):
    in_specs = (
        P("chan", None),
        P("chan", None),
        P("chan", None),
        P("chan", "bl"),
        P("chan", "bl"),
        P(None, "bl"),
    )
    out_specs = (P("chan", None), P("chan", None), P("chan", None))
    return jax.shard_map(body, mesh=mesh, in_specs=in_specs, out_specs=out_specs, check_vma=False)
```

```python
import functools

import jax
import jax.numpy as jnp
import numpy as np
from jax import lax
from jax.experimental import pallas as pl
from jax.experimental.pallas import tpu as pltpu
from jax.sharding import PartitionSpec as P

SKY_DIRECTIONS = 4
ITERS = 2
MU = 0.02
RHO = 25.0

CH = 8
SPAN = 256
ROWS = 8
MESH = pl.DeviceIdType.MESH
FAR_FIRST = (4, 3, 5, 2, 6, 1, 7)
XC_FAR_FIRST = ((2, 1), (2, 0), (1, 1), (3, 1), (1, 0), (3, 0), (0, 1))
f32 = jnp.float32
bf16 = jnp.bfloat16


def basis_coefficients(count):
    t = (2.0 * np.arange(count) - (count - 1)) / count
    columns, result = [], []
    for power in range(4):
        vector = t**power
        for prior in columns:
            vector = vector - np.sum(prior * vector) * prior
        vector = vector / np.sqrt(np.sum(vector * vector))
        columns.append(vector)
        powers = list(range(power % 2, power + 1, 2))
        fit = np.linalg.lstsq(np.stack([t**p for p in powers], 1), vector, rcond=None)[0]
        row = [0.0] * 4
        for p, value in zip(powers, fit):
            row[p] = float(value)
        result.append(row)
    return result


def basis_at(coefficients, channel, count):
    t = (2.0 * channel.astype(f32) - (count - 1)) / count
    t2 = t * t
    c = coefficients
    return (
        jnp.full_like(t, c[0][0]),
        c[1][1] * t,
        c[2][2] * t2 + c[2][0],
        (c[3][3] * t2 + c[3][1]) * t,
    )


def two_pieces(x):
    hi = x.astype(bf16)
    return hi, (x - hi.astype(f32)).astype(bf16)


def three_pieces(x):
    hi = x.astype(bf16)
    rest = x - hi.astype(f32)
    mid = rest.astype(bf16)
    return hi, mid, (rest - mid.astype(f32)).astype(bf16)


def pick(one_hot, x):
    return sum(jnp.dot(one_hot, piece, preferred_element_type=f32) for piece in three_pieces(x))


def iota(shape, dim):
    return lax.broadcasted_iota(jnp.int32, shape, dim)


def working_to_given(n):
    pol, row, chan = n // 64, (n // 8) % 8, n % 8
    return chan * 16 + (row // 2) * 4 + pol * 2 + row % 2


def pair_terms(near, far, model, seen_r, seen_i):
    total_r, total_i = -seen_r, -seen_i
    rows = [slice(8 * i, 8 * i + 8) for i in range(8)]
    first = []
    for k in range(SKY_DIRECTIONS):
        re, im = rows[2 * k], rows[2 * k + 1]
        ar, ai, dr, di, cr, ci = near[re], near[im], far[re], far[im], model[re], model[im]
        er = cr * dr + ci * di
        ei = ci * dr - cr * di
        total_r = total_r + (ar * er - ai * ei)
        total_i = total_i + (ar * ei + ai * er)
        first.append((er, ei))
    near_term, far_term = [], []
    for k in range(SKY_DIRECTIONS):
        re, im = rows[2 * k], rows[2 * k + 1]
        ar, ai, cr, ci = near[re], near[im], model[re], model[im]
        er, ei = first[k]
        fr = ar * cr - ai * ci
        fi = ar * ci + ai * cr
        near_term += [total_r * er + total_i * ei, total_i * er - total_r * ei]
        far_term += [total_r * fr + total_i * fi, total_r * fi - total_i * fr]
    return jnp.concatenate(near_term, 0), jnp.concatenate(far_term, 0)


def kernel(
    count,
    coefficients,
    g_hbm, z_hbm, u_hbm, c_hbm, v_hbm, s_hbm,
    g_out, z_out, u_out,
    g_in, z_in, u_in, c_in, v_in, s_in,
    hot, hot_t, model, seen,
    grad, grad_land, half, half_land, gains, part_z, part_x, weights,
    in_sem, rs_s, rs_r, zh_s, zh_r, ag_s, ag_r, pz_s, pz_r, px_s, px_r, aw_s, aw_r,
):
    width = s_in.shape[1]
    stations = g_in.shape[1]
    lanes = stations // 2

    chan, bl = lax.axis_index("chan"), lax.axis_index("bl")
    core, z_lo, x = chan % 2, (chan // 2) % 4, chan // 8
    y, z_hi = bl % 8, bl // 8
    zz, xc = z_hi * 4 + z_lo, x * 2 + core

    def y_peer(d):
        return (chan, z_hi * 8 + (y + d) % 8)

    def z_peer(d):
        other = (zz + d) % 8
        return ((x * 4 + other % 4) * 2 + core, (other // 4) * 8 + y)

    def xc_peer(dx, dc):
        return ((((x + dx) % 4) * 4 + z_lo) * 2 + (core + dc) % 2, bl)

    loads = [
        pltpu.make_async_copy(src, dst, in_sem.at[i])
        for i, (src, dst) in enumerate(
            ((s_hbm, s_in), (g_hbm, g_in), (c_hbm, c_in), (v_hbm, v_in), (z_hbm, z_in), (u_hbm, u_in))
        )
    ]
    for load in loads:
        load.start()

    barrier = pltpu.get_barrier_semaphore()
    peers = [y_peer(d) for d in FAR_FIRST] + [z_peer(d) for d in FAR_FIRST] + [xc_peer(*d) for d in XC_FAR_FIRST]
    for peer in peers:
        pl.semaphore_signal(barrier, inc=1, device_id=peer, device_id_type=MESH)

    sent = []

    def send(src, dst, send_sem, recv_sem, peer):
        copy = pltpu.make_async_remote_copy(
            src_ref=src, dst_ref=dst, send_sem=send_sem, recv_sem=recv_sem, device_id=peer, device_id_type=MESH
        )
        copy.start()
        sent.append(copy)
        return copy

    loads[0].wait()
    for end in range(2):
        ids = s_in[end : end + 1, :]
        for low in range(0, stations, SPAN):
            local = jnp.where((ids >= low) & (ids < low + SPAN), ids - low, -1).astype(f32).astype(bf16)
            hot[low : low + SPAN, end * width : (end + 1) * width] = jnp.where(
                iota((SPAN, 1), 0).astype(f32).astype(bf16) == local, jnp.ones((), bf16), jnp.zeros((), bf16)
            )
    for load in loads[1:4]:
        load.wait()
    column = jnp.transpose(s_in[...].astype(f32))
    for end in range(2):
        for low in range(0, stations, SPAN):
            local = column[:, end : end + 1] - low
            local = jnp.where((local >= 0.0) & (local < SPAN), local, -1.0)
            local = jnp.broadcast_to(local, (width, 128)).astype(bf16)
            for lane in range(0, SPAN, 128):
                hot_t[end * width : (end + 1) * width, low + lane : low + lane + 128] = jnp.where(
                    (iota((1, 128), 1) + lane).astype(f32).astype(bf16) == local, jnp.ones((), bf16), jnp.zeros((), bf16)
                )

    turn = jnp.where(working_to_given(iota((128, 128), 0)) == iota((128, 128), 1), 1.0, 0.0).astype(bf16)
    g_hi, g_lo = (jnp.dot(turn, piece, preferred_element_type=f32).astype(bf16) for piece in two_pieces(g_in[...]))
    turned = jnp.dot(turn, c_in[...], preferred_element_type=f32)
    for pol in range(2):
        model[pol] = turned[64 * pol : 64 * pol + 64]
    seen_rows = iota((32, 32), 0)
    seen_turn = jnp.where((seen_rows % 8) * 4 + seen_rows // 8 == iota((32, 32), 1), 1.0, 0.0).astype(bf16)
    turned = pick(seen_turn, v_in[...])
    for row in range(4):
        seen[row] = turned[8 * row : 8 * row + 8]

    def gradient(it, pol):
        if it == 0:
            lhs = jnp.concatenate([g_hi[64 * pol : 64 * pol + 64], g_lo[64 * pol : 64 * pol + 64]], 0)
        else:
            lhs = jnp.concatenate(two_pieces(gains[it - 1, pol].reshape(64, stations)), 0)
        near = jnp.dot(lhs, hot[:, :width], preferred_element_type=f32)
        far = jnp.dot(lhs, hot[:, width:], preferred_element_type=f32)
        near_term, far_term = pair_terms(
            near[:64] + near[64:], far[:64] + far[64:], model[pol], seen[2 * pol], seen[2 * pol + 1]
        )
        total = jnp.dot(jnp.concatenate(two_pieces(near_term), 0), hot_t[:width], preferred_element_type=f32) + jnp.dot(
            jnp.concatenate(two_pieces(far_term), 0), hot_t[width:], preferred_element_type=f32
        )
        grad[it, pol] = (total[:64] + total[64:]).reshape(ROWS, CH, stations)

    def scatter_rows(it, pol):
        return [
            send(
                grad.at[it, pol, (y + d) % 8], grad_land.at[it, pol, i], rs_s.at[it, pol, i], rs_r.at[it, pol, i], y_peer(d)
            )
            for i, d in enumerate(FAR_FIRST)
        ]

    own_basis = basis_at(coefficients, chan * CH + iota((CH, 1), 0), count)
    first_z = jnp.where(z_hi == 0, 1.0, 0.0)

    def take(it, pol, copies):
        arrived(copies)
        total = grad[it, pol, y]
        for i in range(7):
            total = total + grad_land[it, pol, i]
        half[it, pol] = total
        return total

    def pair(it, pol):
        return send(half.at[it, pol], half_land.at[it, pol], zh_s.at[it, pol], zh_r.at[it, pol], z_peer(4))

    def finish(it, pol, copy, base):
        copy.wait_recv()
        new = base - MU * (half[it, pol] + half_land[it, pol])
        gains[it, pol, y] = new
        return new, [
            send(gains.at[it, pol, y], gains.at[it, pol, y], ag_s.at[it, pol, i], ag_r.at[it, pol, i], y_peer(d))
            for i, d in enumerate(FAR_FIRST)
        ]

    def coefficient_rows(part):
        row = iota((8, lanes), 0)
        result = jnp.zeros((8, lanes), f32)
        for r, b in enumerate(own_basis):
            total = jnp.sum(b * part, axis=0, keepdims=True)
            for h in range(2):
                result = jnp.where(row == 4 * h + r, total[:, h * lanes : (h + 1) * lanes], result)
        return result

    def fit_z(it, pol, part):
        part_z[it, pol, zz] = coefficient_rows(part)
        mine = part_z.at[it, pol, zz]
        return [
            send(mine, mine, pz_s.at[it, pol, i], pz_r.at[it, pol, i], z_peer(d)) for i, d in enumerate(FAR_FIRST)
        ]

    def fit_xc(it, pol, copies):
        arrived(copies)
        part_x[it, pol, xc] = total_of(part_z, it, pol)
        mine = part_x.at[it, pol, xc]
        return [
            send(mine, mine, px_s.at[it, pol, i], px_r.at[it, pol, i], xc_peer(*d)) for i, d in enumerate(XC_FAR_FIRST)
        ]

    def fit_done(it, pol, copies):
        arrived(copies)
        total = total_of(part_x, it, pol)
        weights[it, pol, y] = total
        return total

    def spread(it, pol):
        mine = weights.at[it, pol, y]
        return [
            send(mine, mine, aw_s.at[it, pol, i], aw_r.at[it, pol, i], y_peer(d)) for i, d in enumerate(FAR_FIRST)
        ]

    def total_of(parts, it, pol):
        total = parts[it, pol, 0]
        for i in range(1, 8):
            total = total + parts[it, pol, i]
        return total

    def arrived(copies):
        for copy in copies:
            copy.wait_recv()

    gradient(0, 0)
    pl.semaphore_wait(barrier, len(peers))
    rows0 = [scatter_rows(0, 0)]
    gradient(0, 1)
    rows0.append(scatter_rows(0, 1))

    loads[4].wait()
    loads[5].wait()
    own_rows = iota((16, 128), 0)
    own_turn = jnp.where(
        (own_rows % 8) * 16 + (y // 2) * 4 + (own_rows // 8) * 2 + y % 2 == iota((16, 128), 1), 1.0, 0.0
    ).astype(bf16)
    kept = g_in[...] - MU * RHO * (g_in[...] - z_in[...] + u_in[...])
    base0, dual0 = pick(own_turn, kept), pick(own_turn, u_in[...])
    base0 = [base0[8 * pol : 8 * pol + 8] for pol in range(2)]
    dual0 = [dual0[8 * pol : 8 * pol + 8] for pol in range(2)]

    pairs = []
    totals = [take(0, 0, rows0[0])]
    pairs.append(pair(0, 0))
    totals.append(take(0, 1, rows0[1]))
    pairs.append(pair(0, 1))
    fits = [fit_z(0, pol, first_z * (base0[pol] + dual0[pol]) - MU * totals[pol]) for pol in range(2)]
    done = [finish(0, 0, pairs[0], base0[0])]
    done.append(finish(0, 1, pairs[1], base0[1]))

    arrived(done[0][1])
    gradient(1, 0)
    rows1 = [scatter_rows(1, 0)]
    fits = [fit_xc(0, pol, fits[pol]) for pol in range(2)]
    arrived(done[1][1])
    gradient(1, 1)
    rows1.append(scatter_rows(1, 1))

    base1, fixed1 = [], []
    for pol in range(2):
        weight = fit_done(0, pol, fits[pol])
        fitted = jnp.concatenate(
            [sum(own_basis[r] * weight[4 * h + r : 4 * h + r + 1, :] for r in range(4)) for h in range(2)], 1
        )
        new = done[pol][0]
        dual1 = dual0[pol] + new - fitted
        base1.append(new - MU * RHO * (new - fitted + dual1))
        fixed1.append(first_z * (base1[pol] + dual1))

    back = jnp.where(working_to_given(iota((128, 128), 1)) == iota((128, 128), 0), 1.0, 0.0).astype(bf16)
    given = iota((128, 1), 0)
    given_row = ((given // 2) % 2) * 8 + ((given // 4) % 4) * 2 + given % 2
    values = basis_at(coefficients, chan * CH + given // 16, count)
    slot = iota((1, 128), 1)
    spans = []
    for h in range(2):
        span = jnp.where(
            (slot // 8 == given_row) & ((slot // 4) % 2 == h),
            sum(jnp.where(slot % 4 == r, values[r], 0.0) for r in range(4)),
            0.0,
        )
        span_hi, span_lo = two_pieces(span)
        spans.append(jnp.concatenate([span_hi, span_hi, span_lo, span_lo], 1))

    def evaluate(it):
        hi, lo = two_pieces(weights[it].reshape(128, lanes))
        pieces = jnp.concatenate([hi, lo, hi, lo], 0)
        return jnp.concatenate([jnp.dot(span, pieces, preferred_element_type=f32) for span in spans], 1)

    u_out[...] = u_in[...] + pick(back, gains[0].reshape(128, stations))

    pairs, fits = [], []
    for pol in range(2):
        total = take(1, pol, rows1[pol])
        fits.append(fit_z(1, pol, fixed1[pol] - MU * total))
        pairs.append(pair(1, pol))
    spreads = spread(0, 0) + spread(0, 1)
    done = [finish(1, 0, pairs[0], base1[0])[1]]
    fits = [fit_xc(1, pol, fits[pol]) for pol in range(2)]
    done.append(finish(1, 1, pairs[1], base1[1])[1])
    arrived(spreads)
    u_out[...] = u_out[...] - evaluate(0)
    spreads = []
    for pol in range(2):
        fit_done(1, pol, fits[pol])
        spreads += spread(1, pol)
    for copies in done:
        arrived(copies)
    g_new = pick(back, gains[1].reshape(128, stations))
    g_out[...] = g_new
    u_out[...] = u_out[...] + g_new
    for copy in sent[: -len(spreads)]:
        copy.wait_send()
    arrived(spreads)
    fitted = evaluate(1)
    z_out[...] = fitted
    u_out[...] = u_out[...] - fitted
    for copy in spreads:
        copy.wait_send()


def store(*refs):
    n = len(refs) // 2
    copies = [pltpu.make_async_copy(refs[i], refs[n + i], refs[-1].at[i]) for i in range(n)]
    for copy in copies:
        copy.start()
    for copy in copies:
        copy.wait()


def body(gains, consensus, dual, coherence, visibility, stations):
    rows, sites = gains.shape
    width = coherence.shape[1]
    count = rows // 16 * lax.axis_size("chan")
    vmem = pltpu.VMEM
    dma = pltpu.SemaphoreType.DMA
    out = jax.ShapeDtypeStruct((rows, sites), f32)
    results = pl.pallas_call(
        functools.partial(kernel, count, basis_coefficients(count)),
        out_shape=(pltpu.VMEM((rows, sites), f32),) * 3,
        in_specs=[pl.BlockSpec(memory_space=pltpu.HBM)] * 6,
        out_specs=tuple([pl.BlockSpec(memory_space=pltpu.VMEM)] * 3),
        scratch_shapes=[
            vmem((rows, sites), f32),
            vmem((rows, sites), f32),
            vmem((rows, sites), f32),
            vmem((rows, width), bf16),
            vmem((rows // 4, width), f32),
            vmem((2, width), jnp.int32),
            vmem((sites, 2 * width), bf16),
            vmem((2 * width, sites), bf16),
            vmem((2, 64, width), f32),
            vmem((4, CH, width), f32),
            vmem((ITERS, 2, ROWS, CH, sites), f32),
            vmem((ITERS, 2, 7, CH, sites), f32),
            vmem((ITERS, 2, CH, sites), f32),
            vmem((ITERS, 2, CH, sites), f32),
            vmem((ITERS, 2, ROWS, CH, sites), f32),
            vmem((ITERS, 2, 8, 8, sites // 2), f32),
            vmem((ITERS, 2, 8, 8, sites // 2), f32),
            vmem((ITERS, 2, 8, 8, sites // 2), f32),
            dma((6,)),
            dma((ITERS, 2, 7)),
            dma((ITERS, 2, 7)),
            dma((ITERS, 2)),
            dma((ITERS, 2)),
            dma((ITERS, 2, 7)),
            dma((ITERS, 2, 7)),
            dma((ITERS, 2, 7)),
            dma((ITERS, 2, 7)),
            dma((ITERS, 2, 7)),
            dma((ITERS, 2, 7)),
            dma((ITERS, 2, 7)),
            dma((ITERS, 2, 7)),
        ],
        compiler_params=pltpu.CompilerParams(collective_id=0, has_side_effects=True, vmem_limit_bytes=44 << 20),
    )(*(pltpu.with_memory_space_constraint(x, pltpu.HBM) for x in (gains, consensus, dual, coherence, visibility, stations)))
    return pl.pallas_call(
        store,
        out_shape=(out, out, out),
        in_specs=[pl.BlockSpec(memory_space=pltpu.VMEM)] * 3,
        out_specs=tuple([pl.BlockSpec(memory_space=pl.ANY)] * 3),
        scratch_shapes=[dma((3,))],
    )(*(pltpu.with_memory_space_constraint(x, pltpu.VMEM) for x in results))


def solution(mesh):
    in_specs = (
        P("chan", None),
        P("chan", None),
        P("chan", None),
        P("chan", "bl"),
        P("chan", "bl"),
        P(None, "bl"),
    )
    out_specs = (P("chan", None), P("chan", None), P("chan", None))
    return jax.shard_map(body, mesh=mesh, in_specs=in_specs, out_specs=out_specs, check_vma=False)
```

```python
import functools

import jax
import jax.numpy as jnp
import numpy as np
from jax import lax
from jax.experimental import pallas as pl
from jax.experimental.pallas import tpu as pltpu
from jax.sharding import PartitionSpec as P

SKY_DIRECTIONS = 4
ITERS = 2
MU = 0.02
RHO = 25.0

CH = 8
SPAN = 256
ROWS = 8
MESH = pl.DeviceIdType.MESH
FAR_FIRST = (4, 3, 5, 2, 6, 1, 7)
XC_FAR_FIRST = ((2, 1), (2, 0), (1, 1), (3, 1), (1, 0), (3, 0), (0, 1))
f32 = jnp.float32
bf16 = jnp.bfloat16


def basis_coefficients(count):
    t = (2.0 * np.arange(count) - (count - 1)) / count
    columns, result = [], []
    for power in range(4):
        vector = t**power
        for prior in columns:
            vector = vector - np.sum(prior * vector) * prior
        vector = vector / np.sqrt(np.sum(vector * vector))
        columns.append(vector)
        powers = list(range(power % 2, power + 1, 2))
        fit = np.linalg.lstsq(np.stack([t**p for p in powers], 1), vector, rcond=None)[0]
        row = [0.0] * 4
        for p, value in zip(powers, fit):
            row[p] = float(value)
        result.append(row)
    return result


def basis_at(coefficients, channel, count):
    t = (2.0 * channel.astype(f32) - (count - 1)) / count
    t2 = t * t
    c = coefficients
    return (
        jnp.full_like(t, c[0][0]),
        c[1][1] * t,
        c[2][2] * t2 + c[2][0],
        (c[3][3] * t2 + c[3][1]) * t,
    )


def two_pieces(x):
    hi = x.astype(bf16)
    return hi, (x - hi.astype(f32)).astype(bf16)


def three_pieces(x):
    hi = x.astype(bf16)
    rest = x - hi.astype(f32)
    mid = rest.astype(bf16)
    return hi, mid, (rest - mid.astype(f32)).astype(bf16)


def pick(one_hot, x):
    return sum(jnp.dot(one_hot, piece, preferred_element_type=f32) for piece in three_pieces(x))


def iota(shape, dim):
    return lax.broadcasted_iota(jnp.int32, shape, dim)


def working_to_given(n):
    pol, row, chan = n // 64, (n // 8) % 8, n % 8
    return chan * 16 + (row // 2) * 4 + pol * 2 + row % 2


def pair_terms(near, far, model, seen_r, seen_i):
    total_r, total_i = -seen_r, -seen_i
    rows = [slice(8 * i, 8 * i + 8) for i in range(8)]
    first = []
    for k in range(SKY_DIRECTIONS):
        re, im = rows[2 * k], rows[2 * k + 1]
        ar, ai, dr, di, cr, ci = near[re], near[im], far[re], far[im], model[re], model[im]
        er = cr * dr + ci * di
        ei = ci * dr - cr * di
        total_r = total_r + (ar * er - ai * ei)
        total_i = total_i + (ar * ei + ai * er)
        first.append((er, ei))
    near_term, far_term = [], []
    for k in range(SKY_DIRECTIONS):
        re, im = rows[2 * k], rows[2 * k + 1]
        ar, ai, cr, ci = near[re], near[im], model[re], model[im]
        er, ei = first[k]
        fr = ar * cr - ai * ci
        fi = ar * ci + ai * cr
        near_term += [total_r * er + total_i * ei, total_i * er - total_r * ei]
        far_term += [total_r * fr + total_i * fi, total_r * fi - total_i * fr]
    return jnp.concatenate(near_term, 0), jnp.concatenate(far_term, 0)


def kernel(
    count,
    coefficients,
    g_hbm, z_hbm, u_hbm, c_hbm, v_hbm, s_hbm,
    g_out, z_out, u_out,
    g_in, z_in, u_in, c_in, v_in, s_in,
    hot, hot_t, model, seen,
    grad, grad_land, half, half_land, gains, part_z, part_x, weights,
    in_sem, rs_s, rs_r, zh_s, zh_r, ag_s, ag_r, pz_s, pz_r, px_s, px_r, aw_s, aw_r,
):
    width = s_in.shape[1]
    stations = g_in.shape[1]
    lanes = stations // 2

    chan, bl = lax.axis_index("chan"), lax.axis_index("bl")
    core, z_lo, x = chan % 2, (chan // 2) % 4, chan // 8
    y, z_hi = bl % 8, bl // 8
    zz, xc = z_hi * 4 + z_lo, x * 2 + core

    def y_peer(d):
        return (chan, z_hi * 8 + (y + d) % 8)

    def z_peer(d):
        other = (zz + d) % 8
        return ((x * 4 + other % 4) * 2 + core, (other // 4) * 8 + y)

    def xc_peer(dx, dc):
        return ((((x + dx) % 4) * 4 + z_lo) * 2 + (core + dc) % 2, bl)

    loads = [
        pltpu.make_async_copy(src, dst, in_sem.at[i])
        for i, (src, dst) in enumerate(
            ((s_hbm, s_in), (g_hbm, g_in), (c_hbm, c_in), (v_hbm, v_in), (z_hbm, z_in), (u_hbm, u_in))
        )
    ]
    for load in loads:
        load.start()

    barrier = pltpu.get_barrier_semaphore()
    peers = [y_peer(d) for d in FAR_FIRST] + [z_peer(d) for d in FAR_FIRST] + [xc_peer(*d) for d in XC_FAR_FIRST]
    for peer in peers:
        pl.semaphore_signal(barrier, inc=1, device_id=peer, device_id_type=MESH)

    sent = []

    def send(src, dst, send_sem, recv_sem, peer):
        copy = pltpu.make_async_remote_copy(
            src_ref=src, dst_ref=dst, send_sem=send_sem, recv_sem=recv_sem, device_id=peer, device_id_type=MESH
        )
        copy.start()
        sent.append(copy)
        return copy

    loads[0].wait()
    for end in range(2):
        ids = s_in[end : end + 1, :]
        for low in range(0, stations, SPAN):
            local = jnp.where((ids >= low) & (ids < low + SPAN), ids - low, -1).astype(f32).astype(bf16)
            hot[low : low + SPAN, end * width : (end + 1) * width] = jnp.where(
                iota((SPAN, 1), 0).astype(f32).astype(bf16) == local, jnp.ones((), bf16), jnp.zeros((), bf16)
            )
    for load in loads[1:4]:
        load.wait()
    column = jnp.transpose(s_in[...].astype(f32))
    for end in range(2):
        for low in range(0, stations, SPAN):
            local = column[:, end : end + 1] - low
            local = jnp.where((local >= 0.0) & (local < SPAN), local, -1.0)
            local = jnp.broadcast_to(local, (width, 128)).astype(bf16)
            for lane in range(0, SPAN, 128):
                hot_t[end * width : (end + 1) * width, low + lane : low + lane + 128] = jnp.where(
                    (iota((1, 128), 1) + lane).astype(f32).astype(bf16) == local, jnp.ones((), bf16), jnp.zeros((), bf16)
                )

    turn = jnp.where(working_to_given(iota((128, 128), 0)) == iota((128, 128), 1), 1.0, 0.0).astype(bf16)
    g_hi, g_lo = (jnp.dot(turn, piece, preferred_element_type=f32).astype(bf16) for piece in two_pieces(g_in[...]))
    turned = jnp.dot(turn, c_in[...], preferred_element_type=f32)
    for pol in range(2):
        model[pol] = turned[64 * pol : 64 * pol + 64]
    seen_rows = iota((32, 32), 0)
    seen_turn = jnp.where((seen_rows % 8) * 4 + seen_rows // 8 == iota((32, 32), 1), 1.0, 0.0).astype(bf16)
    turned = pick(seen_turn, v_in[...])
    for row in range(4):
        seen[row] = turned[8 * row : 8 * row + 8]

    def gradient(it, pol):
        if it == 0:
            lhs = jnp.concatenate([g_hi[64 * pol : 64 * pol + 64], g_lo[64 * pol : 64 * pol + 64]], 0)
        else:
            lhs = jnp.concatenate(two_pieces(gains[it - 1, pol].reshape(64, stations)), 0)
        near = jnp.dot(lhs, hot[:, :width], preferred_element_type=f32)
        far = jnp.dot(lhs, hot[:, width:], preferred_element_type=f32)
        near_term, far_term = pair_terms(
            near[:64] + near[64:], far[:64] + far[64:], model[pol], seen[2 * pol], seen[2 * pol + 1]
        )
        total = jnp.dot(jnp.concatenate(two_pieces(near_term), 0), hot_t[:width], preferred_element_type=f32) + jnp.dot(
            jnp.concatenate(two_pieces(far_term), 0), hot_t[width:], preferred_element_type=f32
        )
        grad[it, pol] = (total[:64] + total[64:]).reshape(ROWS, CH, stations)

    def scatter_rows(it, pol):
        return [
            send(
                grad.at[it, pol, (y + d) % 8], grad_land.at[it, pol, i], rs_s.at[it, pol, i], rs_r.at[it, pol, i], y_peer(d)
            )
            for i, d in enumerate(FAR_FIRST)
        ]

    own_basis = basis_at(coefficients, chan * CH + iota((CH, 1), 0), count)
    first_z = jnp.where(z_hi == 0, 1.0, 0.0)

    def take(it, pol, copies):
        arrived(copies)
        total = grad[it, pol, y]
        for i in range(7):
            total = total + grad_land[it, pol, i]
        half[it, pol] = total
        return total

    def pair(it, pol):
        return send(half.at[it, pol], half_land.at[it, pol], zh_s.at[it, pol], zh_r.at[it, pol], z_peer(4))

    def finish(it, pol, copy, base):
        copy.wait_recv()
        new = base - MU * (half[it, pol] + half_land[it, pol])
        gains[it, pol, y] = new
        return new, [
            send(gains.at[it, pol, y], gains.at[it, pol, y], ag_s.at[it, pol, i], ag_r.at[it, pol, i], y_peer(d))
            for i, d in enumerate(FAR_FIRST)
        ]

    def coefficient_rows(part):
        row = iota((8, lanes), 0)
        result = jnp.zeros((8, lanes), f32)
        for r, b in enumerate(own_basis):
            total = jnp.sum(b * part, axis=0, keepdims=True)
            for h in range(2):
                result = jnp.where(row == 4 * h + r, total[:, h * lanes : (h + 1) * lanes], result)
        return result

    def fit_z(it, pol, part):
        part_z[it, pol, zz] = coefficient_rows(part)
        mine = part_z.at[it, pol, zz]
        return [
            send(mine, mine, pz_s.at[it, pol, i], pz_r.at[it, pol, i], z_peer(d)) for i, d in enumerate(FAR_FIRST)
        ]

    def fit_xc(it, pol, copies):
        arrived(copies)
        part_x[it, pol, xc] = total_of(part_z, it, pol)
        mine = part_x.at[it, pol, xc]
        return [
            send(mine, mine, px_s.at[it, pol, i], px_r.at[it, pol, i], xc_peer(*d)) for i, d in enumerate(XC_FAR_FIRST)
        ]

    def fit_done(it, pol, copies):
        arrived(copies)
        total = total_of(part_x, it, pol)
        weights[it, pol, y] = total
        return total

    def spread(it, pol):
        mine = weights.at[it, pol, y]
        return [
            send(mine, mine, aw_s.at[it, pol, i], aw_r.at[it, pol, i], y_peer(d)) for i, d in enumerate(FAR_FIRST)
        ]

    def total_of(parts, it, pol):
        total = parts[it, pol, 0]
        for i in range(1, 8):
            total = total + parts[it, pol, i]
        return total

    def arrived(copies):
        for copy in copies:
            copy.wait_recv()

    gradient(0, 0)
    pl.semaphore_wait(barrier, len(peers))
    rows0 = [scatter_rows(0, 0)]
    gradient(0, 1)
    rows0.append(scatter_rows(0, 1))

    loads[4].wait()
    loads[5].wait()
    own_rows = iota((16, 128), 0)
    own_turn = jnp.where(
        (own_rows % 8) * 16 + (y // 2) * 4 + (own_rows // 8) * 2 + y % 2 == iota((16, 128), 1), 1.0, 0.0
    ).astype(bf16)
    kept = g_in[...] - MU * RHO * (g_in[...] - z_in[...] + u_in[...])
    base0, dual0 = pick(own_turn, kept), pick(own_turn, u_in[...])
    base0 = [base0[8 * pol : 8 * pol + 8] for pol in range(2)]
    dual0 = [dual0[8 * pol : 8 * pol + 8] for pol in range(2)]

    pairs = []
    totals = [take(0, 0, rows0[0])]
    pairs.append(pair(0, 0))
    totals.append(take(0, 1, rows0[1]))
    pairs.append(pair(0, 1))
    fits = [fit_z(0, pol, first_z * (base0[pol] + dual0[pol]) - MU * totals[pol]) for pol in range(2)]
    done = [finish(0, 0, pairs[0], base0[0])]
    done.append(finish(0, 1, pairs[1], base0[1]))

    arrived(done[0][1])
    gradient(1, 0)
    rows1 = [scatter_rows(1, 0)]
    fits = [fit_xc(0, pol, fits[pol]) for pol in range(2)]
    arrived(done[1][1])
    gradient(1, 1)
    rows1.append(scatter_rows(1, 1))

    base1, fixed1 = [], []
    for pol in range(2):
        weight = fit_done(0, pol, fits[pol])
        fitted = jnp.concatenate(
            [sum(own_basis[r] * weight[4 * h + r : 4 * h + r + 1, :] for r in range(4)) for h in range(2)], 1
        )
        new = done[pol][0]
        dual1 = dual0[pol] + new - fitted
        base1.append(new - MU * RHO * (new - fitted + dual1))
        fixed1.append(first_z * (base1[pol] + dual1))

    back = jnp.where(working_to_given(iota((128, 128), 1)) == iota((128, 128), 0), 1.0, 0.0).astype(bf16)
    given = iota((128, 1), 0)
    given_row = ((given // 2) % 2) * 8 + ((given // 4) % 4) * 2 + given % 2
    values = basis_at(coefficients, chan * CH + given // 16, count)
    slot = iota((1, 128), 1)
    spans = []
    for h in range(2):
        span = jnp.where(
            (slot // 8 == given_row) & ((slot // 4) % 2 == h),
            sum(jnp.where(slot % 4 == r, values[r], 0.0) for r in range(4)),
            0.0,
        )
        span_hi, span_lo = two_pieces(span)
        spans.append(jnp.concatenate([span_hi, span_hi, span_lo, span_lo], 1))

    def evaluate(it):
        hi, lo = two_pieces(weights[it].reshape(128, lanes))
        pieces = jnp.concatenate([hi, lo, hi, lo], 0)
        return jnp.concatenate([jnp.dot(span, pieces, preferred_element_type=f32) for span in spans], 1)

    u_out[...] = u_in[...] + pick(back, gains[0].reshape(128, stations))

    pairs, fits = [], []
    for pol in range(2):
        total = take(1, pol, rows1[pol])
        fits.append(fit_z(1, pol, fixed1[pol] - MU * total))
        pairs.append(pair(1, pol))
    fits[0] = fit_xc(1, 0, fits[0])
    done = [finish(1, 0, pairs[0], base1[0])[1]]
    spreads = spread(0, 0) + spread(0, 1)
    fits[1] = fit_xc(1, 1, fits[1])
    done.append(finish(1, 1, pairs[1], base1[1])[1])
    arrived(spreads)
    u_out[...] = u_out[...] - evaluate(0)
    spreads = []
    for pol in range(2):
        fit_done(1, pol, fits[pol])
        spreads += spread(1, pol)
    for copies in done:
        arrived(copies)
    g_new = pick(back, gains[1].reshape(128, stations))
    g_out[...] = g_new
    u_out[...] = u_out[...] + g_new
    for copy in sent[: -len(spreads)]:
        copy.wait_send()
    arrived(spreads)
    fitted = evaluate(1)
    z_out[...] = fitted
    u_out[...] = u_out[...] - fitted
    for copy in spreads:
        copy.wait_send()


def store(*refs):
    n = len(refs) // 2
    copies = [pltpu.make_async_copy(refs[i], refs[n + i], refs[-1].at[i]) for i in range(n)]
    for copy in copies:
        copy.start()
    for copy in copies:
        copy.wait()


def body(gains, consensus, dual, coherence, visibility, stations):
    rows, sites = gains.shape
    width = coherence.shape[1]
    count = rows // 16 * lax.axis_size("chan")
    vmem = pltpu.VMEM
    dma = pltpu.SemaphoreType.DMA
    out = jax.ShapeDtypeStruct((rows, sites), f32)
    results = pl.pallas_call(
        functools.partial(kernel, count, basis_coefficients(count)),
        out_shape=(pltpu.VMEM((rows, sites), f32),) * 3,
        in_specs=[pl.BlockSpec(memory_space=pltpu.HBM)] * 6,
        out_specs=tuple([pl.BlockSpec(memory_space=pltpu.VMEM)] * 3),
        scratch_shapes=[
            vmem((rows, sites), f32),
            vmem((rows, sites), f32),
            vmem((rows, sites), f32),
            vmem((rows, width), bf16),
            vmem((rows // 4, width), f32),
            vmem((2, width), jnp.int32),
            vmem((sites, 2 * width), bf16),
            vmem((2 * width, sites), bf16),
            vmem((2, 64, width), f32),
            vmem((4, CH, width), f32),
            vmem((ITERS, 2, ROWS, CH, sites), f32),
            vmem((ITERS, 2, 7, CH, sites), f32),
            vmem((ITERS, 2, CH, sites), f32),
            vmem((ITERS, 2, CH, sites), f32),
            vmem((ITERS, 2, ROWS, CH, sites), f32),
            vmem((ITERS, 2, 8, 8, sites // 2), f32),
            vmem((ITERS, 2, 8, 8, sites // 2), f32),
            vmem((ITERS, 2, 8, 8, sites // 2), f32),
            dma((6,)),
            dma((ITERS, 2, 7)),
            dma((ITERS, 2, 7)),
            dma((ITERS, 2)),
            dma((ITERS, 2)),
            dma((ITERS, 2, 7)),
            dma((ITERS, 2, 7)),
            dma((ITERS, 2, 7)),
            dma((ITERS, 2, 7)),
            dma((ITERS, 2, 7)),
            dma((ITERS, 2, 7)),
            dma((ITERS, 2, 7)),
            dma((ITERS, 2, 7)),
        ],
        compiler_params=pltpu.CompilerParams(collective_id=0, has_side_effects=True, vmem_limit_bytes=44 << 20),
    )(*(pltpu.with_memory_space_constraint(x, pltpu.HBM) for x in (gains, consensus, dual, coherence, visibility, stations)))
    return pl.pallas_call(
        store,
        out_shape=(out, out, out),
        in_specs=[pl.BlockSpec(memory_space=pltpu.VMEM)] * 3,
        out_specs=tuple([pl.BlockSpec(memory_space=pl.ANY)] * 3),
        scratch_shapes=[dma((3,))],
    )(*(pltpu.with_memory_space_constraint(x, pltpu.VMEM) for x in results))


def solution(mesh):
    in_specs = (
        P("chan", None),
        P("chan", None),
        P("chan", None),
        P("chan", "bl"),
        P("chan", "bl"),
        P(None, "bl"),
    )
    out_specs = (P("chan", None), P("chan", None), P("chan", None))
    return jax.shard_map(body, mesh=mesh, in_specs=in_specs, out_specs=out_specs, check_vma=False)
```
